256 devices in a mesh: shard: 8 (over x, core), grp: 32 (over z, y).
Axes of the slice: x: 4, y: 4, z: 8, core: 2. Of those that a mesh axis runs over, the one named last changes fastest.
Arguments:
- sketches: float32 [49152, 1024], P(('shard', 'grp')), may hold values from -6 to 6
- labels: int32 [49152, 1], P(('shard', 'grp')), may hold values from 0 to 7; in each aligned block of 192 rows (0 to 191, 192 to 383, ...) at most 48 rows name the same one
- ranks: int32 [49152], P(('shard', 'grp')), may hold values from 0 to 49151, each once
Outputs:
- highest: float32 [49152], P(('shard', 'grp'))
The draws below stay inside these ranges and needn't reach their ends.
Inputs may be any that keep to these rules, and one draw needn't show every extreme that they name: `labels`: within the 192 sketches of one device no label occurs more than 48 times; some label occurs exactly 48 times. `ranks`: every rank occurs once.
All inputs are finite; a program needn't handle non-finite values.
Results may differ from the reference program's by a relative error of at most 0.0012.
Values may be sent and summed in bfloat16 or wider, within the bound.
No kernel may reach another device: no remote copies, remote signals or barrier semaphores. Data moves between devices by JAX's collectives and lax.ppermute only.
A program may use at most 64 MiB of HBM per device.

```python
import math
import jax
import jax.numpy as jnp
import numpy as np
from jax import lax

D = 1024
ROWS_DEV = 192
CAP = 48
ROWS_ALL = 49152
N_SHARD = 8
N_GRP = 32


def steps_of(stream_key, dims, split, low, largest):
    loudness = 1.0
    for position, parts in split:
        draws = jax.random.uniform(jax.random.fold_in(jax.random.fold_in(stream_key, 6), position), (parts,), jnp.float32, low / len(split), largest / len(split))
        loudness = loudness * jnp.repeat(jnp.exp(draws), dims[position] // parts).reshape((-1,) + (1,) * (len(dims) - 1 - position))
    return loudness


def assign_block(key, own, number, rows, count, top, most, slope):
    ranking = jax.random.permutation(key, count)
    crowded, common = portions_of(count, rows * top, most, slope, True), portions_of(count, rows * top, most, slope, False)
    places = jnp.arange(count)

    def named(lengths, turn):
        used = int((lengths > 0).sum())
        fixed = max(1, used // 4)
        passed = fixed + (places - fixed + turn * (used - fixed)) % max(1, count - fixed)
        return jnp.zeros((count,), jnp.int32).at[ranking[jnp.where(places < fixed, places, passed)]].set(jnp.asarray(lengths, jnp.int32))

    lengths = jnp.where(number % 4 == 0, named(crowded, number // 4), named(common, number - number // 4 - 1))
    mixed = jax.random.permutation(jax.random.fold_in(own, 3), count)
    source_of, receiver = mixed[0:count // 2 * 2:2], mixed[1:count // 2 * 2:2]
    margin = jnp.minimum(lengths[source_of] - 1, most - lengths[receiver]) // 2
    margin = jnp.where((source_of == ranking[0]) | (receiver == ranking[0]) | (lengths[receiver] == 0), 0, jnp.maximum(margin, 0))
    passed = jax.random.randint(jax.random.fold_in(own, 4), (count // 2,), 0, 1 << 20) % (margin + 1)
    lengths = lengths.at[source_of].add(-passed).at[receiver].add(passed)
    items = jnp.searchsorted(jnp.cumsum(lengths), jnp.arange(rows * top), side="right").astype(jnp.int32)
    listing = items.reshape(top, rows).T
    listing = listing[jax.random.permutation(jax.random.fold_in(own, 1), rows)]
    turn = jax.random.randint(jax.random.fold_in(own, 2), (rows, 1), 0, top)
    return jnp.take_along_axis(listing, (jnp.arange(top)[None, :] + turn) % top, axis=1)


def portions_of(count, total, most, slope, full):
    loads = [(1 << 20) // math.isqrt(grade ** slope) + 1 for grade in range(1, count + 1)]
    largest = most if full else min(most, max(-(-total // count), total * loads[0] // sum(loads)))
    least = 1 if total - largest >= count - 1 else 0
    given, rest = [largest] + [least] * (count - 1), total - largest - least * (count - 1)
    while rest > 0:
        candidates = [i for i in range(1, count) if given[i] < largest] or [i for i in range(1, count) if given[i] < most]
        mass, remaining = sum([loads[i] for i in candidates]), rest
        for i in candidates:
            addition = min(most - given[i], max(1, remaining * loads[i] // mass), rest)
            given[i] = given[i] + addition
            rest = rest - addition
    return np.array(given)


def noise(key, shape, deviation, limit, shards=(), kind=jnp.bfloat16):
    entries = deviation * jax.random.normal(key, shape, jnp.float32)
    if shards:
        entries = entries * steps_of(key, shape, shards, -0.22, 0.18)
    return jnp.clip(entries, -limit, limit).astype(kind)


def setup_inputs(seed: int = 0) -> dict:
    arg_keys = jax.random.split(jax.random.key(seed), 4)
    sketches = noise(arg_keys[0], (ROWS_ALL, D), 1.0, 6.0, ((0, 256),), jnp.float32)
    labels_keys = jax.random.split(jax.random.fold_in(arg_keys[1], 1), ROWS_ALL // ROWS_DEV)
    labels_turns = jax.random.permutation(jax.random.fold_in(arg_keys[1], 3), ROWS_ALL // ROWS_DEV)
    labels = jax.vmap(lambda own, number: assign_block(jax.random.fold_in(arg_keys[1], 2), own, number, ROWS_DEV, N_SHARD, 1, CAP, 2))(labels_keys, labels_turns).reshape((ROWS_ALL, 1))
    ranks = jax.random.permutation(arg_keys[2], ROWS_ALL).astype(jnp.int32)
    return {"sketches": sketches, "labels": labels, "ranks": ranks}


def reference(sketches, labels, ranks):
    sum_squares = lax.optimization_barrier(jnp.sum(sketches * sketches, axis=1, keepdims=True))
    unit = (sketches * lax.rsqrt(sum_squares + 1e-06)).astype(jnp.bfloat16)
    label_ids = labels[:, 0]
    ordering = jnp.argsort(label_ids, stable=True).astype(jnp.int32)
    cluster_ids = jnp.arange(N_SHARD, dtype=jnp.int32)
    counts = lax.optimization_barrier(jnp.sum((label_ids[None, :] == cluster_ids[:, None]).astype(jnp.int32), axis=1))
    starts = (jnp.cumsum(counts) - counts).astype(jnp.int32)
    width_max = N_SHARD * N_GRP * CAP
    padded_rows = jnp.concatenate([unit[ordering], jnp.zeros((width_max, D), unit.dtype)], axis=0)
    padded_labels = jnp.concatenate([label_ids[ordering], jnp.full((width_max,), -1, jnp.int32)], axis=0)
    padded_ranks = jnp.concatenate([ranks[ordering], jnp.full((width_max,), -1, jnp.int32)], axis=0)
    padded_anchor = jnp.concatenate([ordering, jnp.full((width_max,), ROWS_ALL, jnp.int32)], axis=0)

    def per_cluster(cluster):
        begin_at = starts[cluster]
        slot_rows = lax.dynamic_slice_in_dim(padded_rows, begin_at, width_max, 0)
        slot_labels = lax.dynamic_slice_in_dim(padded_labels, begin_at, width_max, 0)
        slot_ranks = lax.dynamic_slice_in_dim(padded_ranks, begin_at, width_max, 0)
        slot_anchor = lax.dynamic_slice_in_dim(padded_anchor, begin_at, width_max, 0)
        member = slot_labels == cluster
        scores = jnp.dot(slot_rows, slot_rows.T, preferred_element_type=jnp.float32)
        allowed = member[None, :] & (slot_ranks[None, :] < slot_ranks[:, None])
        best_value = lax.optimization_barrier(jnp.max(jnp.where(allowed, scores, jnp.float32(-1.0)), axis=1))
        target = jnp.where(member, slot_anchor, ROWS_ALL).astype(jnp.int32)
        return (best_value, target)
    values, targets = lax.map(per_cluster, cluster_ids)
    highest = jnp.zeros((ROWS_ALL,), jnp.float32).at[targets.reshape(-1)].set(values.reshape(-1), mode='drop')
    return highest
```

```python
import jax
import jax.numpy as jnp
import numpy as np
from jax import lax
from jax.experimental import pallas as pl
from jax.experimental.pallas import tpu as pltpu
from jax.sharding import Mesh, PartitionSpec as P

AXES = ("x", "core", "z", "y")
SIZES = (4, 2, 8, 4)
ROWS = 192
KEYS = 16
DIM = 1024
FAR = 4.0e9
VMEM = pl.BlockSpec(memory_space=pltpu.VMEM)
SMEM = pl.BlockSpec(memory_space=pltpu.SMEM)


def permutation(move):
    pairs = []
    for source in np.ndindex(*SIZES):
        target = np.array(move(*source)) % np.array(SIZES)
        pairs.append((int(np.ravel_multi_index(source, SIZES)), int(np.ravel_multi_index(tuple(target), SIZES))))
    return pairs


def send(array, move):
    return lax.ppermute(array, AXES, permutation(move))


def call(body, outs, scratch=(), flops=0, spaces=None, count=0, name=None):
    return pl.pallas_call(
        body,
        out_shape=outs,
        in_specs=spaces or [VMEM] * count,
        out_specs=VMEM if isinstance(outs, jax.ShapeDtypeStruct) else [VMEM] * len(outs),
        scratch_shapes=list(scratch),
        compiler_params=pltpu.CompilerParams(vmem_limit_bytes=20 << 20),
        cost_estimate=pl.CostEstimate(flops=flops, bytes_accessed=1 << 20, transcendentals=0),
        name=name,
    )


def column_to_row(column):
    n = column.shape[0]
    diagonal = lax.broadcasted_iota(jnp.int32, (n, n), 0) == lax.broadcasted_iota(jnp.int32, (n, n), 1)
    return jnp.sum(jnp.where(diagonal, column, 0.0), axis=0, keepdims=True)


def row_to_column(row):
    n = row.shape[1]
    diagonal = lax.broadcasted_iota(jnp.int32, (n, n), 0) == lax.broadcasted_iota(jnp.int32, (n, n), 1)
    return jnp.sum(jnp.where(diagonal, row, 0.0), axis=1, keepdims=True)


def normalise_body(sketches, labels, ranks, out):
    values = sketches[...]
    scale = lax.rsqrt(jnp.sum(values * values, axis=1, keepdims=True) + 1e-06)
    out[0:ROWS, :] = (values * scale).astype(jnp.bfloat16)
    label_row = column_to_row(labels[...].astype(jnp.float32))
    rank_row = ranks[...]
    high = (rank_row // 256).astype(jnp.float32)
    low = (rank_row % 256).astype(jnp.float32)
    index = lax.broadcasted_iota(jnp.int32, (KEYS, ROWS), 0)
    rows = jnp.where(index == 0, label_row, jnp.where(index == 1, high, jnp.where(index == 2, low, 0.0)))
    out[ROWS : ROWS + KEYS, :] = jnp.zeros((KEYS, DIM), jnp.bfloat16)
    out[ROWS : ROWS + KEYS, 0:ROWS] = rows.astype(jnp.bfloat16)


def pair_body(core, own, other, out):
    me = core[0]
    first, second = pl.multiple_of(me * ROWS, ROWS), pl.multiple_of((1 - me) * ROWS, ROWS)
    out[pl.ds(first, ROWS), :] = own[0:ROWS, :]
    out[pl.ds(second, ROWS), :] = other[0:ROWS, :]
    mine, theirs = own[ROWS : ROWS + KEYS, :].astype(jnp.float32), other[ROWS : ROWS + KEYS, :].astype(jnp.float32)
    lead, tail = jnp.where(me == 0, mine, theirs), jnp.where(me == 0, theirs, mine)
    out[2 * ROWS : 2 * ROWS + KEYS, :] = jnp.concatenate([lead[0:8], tail[0:8]], axis=0).astype(jnp.bfloat16)


def pick_body(core, both, out):
    me = core[0]
    out[0:ROWS, :] = both[pl.ds(pl.multiple_of(me * ROWS, ROWS), ROWS), :]
    keys = both[2 * ROWS : 2 * ROWS + KEYS, :].astype(jnp.float32)
    chosen = jnp.where(me == 0, keys[0:8], keys[8:16])
    out[ROWS : ROWS + KEYS, :] = jnp.concatenate([chosen, jnp.zeros_like(chosen)], axis=0).astype(jnp.bfloat16)


def key_of(rows):
    return rows[0:1] * 65536.0 + rows[1:2] * 256.0 + rows[2:3]


def bundle_body(a, b, c, d, out):
    columns = []
    for i, block in enumerate((a, b, c, d)):
        out[i * ROWS : (i + 1) * ROWS, :] = block[0:ROWS, :]
        keys = block[ROWS : ROWS + KEYS, 0:256].astype(jnp.float32)[0:8]
        columns.append(jnp.transpose(keys)[0:ROWS])
    rows = jnp.transpose(jnp.concatenate(columns, axis=0))
    out[4 * ROWS : 4 * ROWS + KEYS, :] = jnp.zeros((KEYS, DIM), jnp.bfloat16)
    out[4 * ROWS : 4 * ROWS + KEYS, 0 : 4 * ROWS] = jnp.concatenate([rows, jnp.zeros_like(rows)], axis=0).astype(jnp.bfloat16)


def score(queries, bundles, name):
    refs, layout = [], []
    for bundle in bundles:
        layout.append(len(bundle))
        refs += bundle
    blocks = [q.shape[0] // ROWS for q in queries]
    total = sum(blocks)

    def body(*args):
        q_refs, k_refs, out = args[: len(queries)], list(args[len(queries) : -1]), args[-1]
        parts = []
        for n in layout:
            if n == 1:
                (whole,) = k_refs[:1]
                key_rows = whole[4 * ROWS : 4 * ROWS + KEYS, 0 : 4 * ROWS]
                pieces = [(whole, 256 * j, 256) for j in range(3)]
            else:
                top, bottom = k_refs[:2]
                key_rows = bottom[2 * ROWS : 2 * ROWS + KEYS, 0 : 4 * ROWS]
                pieces = [(top, 0, 384), (bottom, 0, 384)]
            k_refs = k_refs[n:]
            key = key_of(key_rows.astype(jnp.float32)[0:8])
            offset = 0
            for ref, start, length in pieces:
                parts.append((ref, start, length, key[:, offset : offset + length]))
                offset += length
        row = 0
        for q_ref, count in zip(q_refs, blocks):
            size = count * ROWS
            keys = q_ref[size : size + KEYS, 0:256].astype(jnp.float32)
            key_q = jnp.concatenate([jnp.transpose(keys[8 * i : 8 * i + 8])[0:ROWS] for i in range(count)], axis=0)
            key_q = key_q[:, 0:1] * 65536.0 + key_q[:, 1:2] * 256.0 + key_q[:, 2:3]
            base = jnp.floor(key_q * (1.0 / 65536.0)) * 65536.0
            best = jnp.full((size, 128), -1.0, jnp.float32)
            for ref, start, length, key_k in parts:
                scores = lax.dot_general(
                    q_ref[0:size, :], ref[start : start + length, :], (((1,), (1,)), ((), ())), preferred_element_type=jnp.float32
                )
                allowed = (key_k < key_q) & (key_k >= base)
                scores = jnp.where(allowed, scores, -1.0)
                for j in range(0, length, 128):
                    best = jnp.maximum(best, scores[:, j : j + 128])
            top = jnp.max(best, axis=1, keepdims=True)
            for i in range(count):
                out[row : row + 1, :] = column_to_row(top[i * ROWS : (i + 1) * ROWS])
                row += 1

    flops = 2 * DIM * ROWS * ROWS * total * 4 * len(bundles)
    return call(body, jax.ShapeDtypeStruct((total, ROWS), jnp.float32), flops=flops, count=len(queries) + len(refs), name=name)(
        *queries, *refs
    )


def on_device(sketches, labels, ranks):
    block_shape = jax.ShapeDtypeStruct((ROWS + KEYS, DIM), jnp.bfloat16)
    pair_shape = jax.ShapeDtypeStruct((2 * ROWS + KEYS, DIM), jnp.bfloat16)
    bundle_shape = jax.ShapeDtypeStruct((4 * ROWS + KEYS, DIM), jnp.bfloat16)
    core = lax.axis_index("core").astype(jnp.int32)
    z = lax.axis_index("z").astype(jnp.int32)
    place = jnp.stack([core, z])
    own = call(normalise_body, block_shape, count=3, name="normalise")(sketches, labels, ranks.reshape(1, ROWS))

    def first(step):
        return lambda x, c, z, y: (x + step * (1 - c), c, z, y + step * c)

    def second(step):
        return lambda x, c, z, y: (x + step * c, c, z, y + step * (1 - c))

    def along_z(x, c, z, y):
        return (x, c, z + 1 - 2 * c, y)

    def across(x, c, z, y):
        return (x, c + 1, z, y)

    partner = send(own, across)
    line = [own, send(own, first(1)), send(own, first(-1)), send(own, first(2))]
    here = call(pair_body, pair_shape, spaces=[SMEM, VMEM, VMEM], name="pair")(place, own, partner)
    near = send(here, along_z)
    near_other = send(near, across)
    bundle = call(bundle_body, bundle_shape, count=4, name="bundle")(*line)
    after, before = send(bundle, second(-1)), send(bundle, second(1))
    middle = send(near, along_z)
    middle_other = send(middle, across)
    opposite = [send(before[0 : 2 * ROWS], second(1)), send(after[2 * ROWS :], second(-1))]
    far = send(middle, along_z)
    far_other = send(far, across)
    last = send(call(pick_body, block_shape, spaces=[SMEM, VMEM], name="pick")(place, far), along_z)
    last_other = send(last, across)

    s0 = score([here], [[bundle]], "s0")
    s1 = score([near, near_other], [[bundle]], "s1")
    s2 = score([middle, middle_other], [[bundle]], "s2")
    s3 = score([here, near, near_other], [[after], [before]], "s3")
    s4 = score([middle, middle_other], [[after], [before]], "s4")
    s5 = score([far, far_other], [[bundle], [after], [before]], "s5")
    s6 = score([here, near, near_other, middle, middle_other, far, far_other], [opposite], "s6")
    s7 = score([last, last_other], [[bundle], [after], [before], opposite], "s7")

    def merge_body(at, s0, s1, s2, s3, s4, s5, s6, s7, out):
        me, level = at[0], at[1]
        six = s6[...]
        group = {
            0: jnp.maximum(jnp.maximum(s0[...], s3[0:2]), six[0:2]),
            1: jnp.maximum(jnp.maximum(s1[...], s3[2:6]), six[2:6]),
            2: jnp.maximum(jnp.maximum(s2[...], s4[...]), six[6:10]),
            3: jnp.maximum(s5[...], six[10:14]),
        }

        def put(level_of, which, row):
            out[pl.ds(which * 8 + lax.rem(level_of + 16, 8), 1), :] = row

        sign = 2 * me - 1
        put(level, 0, group[0][0:1])
        put(level, 1, group[0][1:2])
        for k in (1, 2, 3):
            put(level + sign * k, 0, group[k][0:1])
            put(level + sign * k, 1, group[k][1:2])
            put(level - sign * k, 0, group[k][2:3])
            put(level - sign * k, 1, group[k][3:4])
        put(level + 4, me, s7[0:1])
        put(level + 4, 1 - me, s7[1:2])

    partial = call(
        merge_body, jax.ShapeDtypeStruct((16, ROWS), jnp.float32), spaces=[SMEM] + [VMEM] * 8, name="merge"
    )(place, s0, s1, s2, s3, s4, s5, s6, s7)
    returned = lax.all_to_all(partial, ("core", "z"), split_axis=0, concat_axis=0, tiled=True)
    return jnp.max(returned, axis=0)


def solution(mesh):
    fine = Mesh(mesh.devices.reshape(SIZES), AXES)
    return jax.shard_map(
        on_device,
        mesh=fine,
        in_specs=(P(AXES, None), P(AXES, None), P(AXES)),
        out_specs=P(AXES),
        check_vma=False,
    )
```

```python
import jax
import jax.numpy as jnp
import numpy as np
from jax import lax
from jax.experimental import pallas as pl
from jax.experimental.pallas import tpu as pltpu
from jax.sharding import Mesh, PartitionSpec as P

AXES = ("x", "core", "z", "y")
SIZES = (4, 2, 8, 4)
ROWS = 192
WEIGHT = 1
KEYS = 16
DIM = 1024
VMEM = pl.BlockSpec(memory_space=pltpu.VMEM)
HBM = pl.BlockSpec(memory_space=pltpu.HBM)
SMEM = pl.BlockSpec(memory_space=pltpu.SMEM)


def permutation(move):
    pairs = []
    for source in np.ndindex(*SIZES):
        target = np.array(move(*source)) % np.array(SIZES)
        pairs.append((int(np.ravel_multi_index(source, SIZES)), int(np.ravel_multi_index(tuple(target), SIZES))))
    return pairs


def send(array, move, name):
    with jax.named_scope(name):
        return lax.ppermute(array, AXES, permutation(move))


def call(body, outs, scratch=(), flops=0, spaces=None, count=0, name=None, vmem=10):
    return pl.pallas_call(
        body,
        out_shape=outs,
        in_specs=spaces or [VMEM] * count,
        out_specs=VMEM if isinstance(outs, jax.ShapeDtypeStruct) else [VMEM] * len(outs),
        scratch_shapes=list(scratch),
        compiler_params=pltpu.CompilerParams(vmem_limit_bytes=vmem << 20),
        cost_estimate=pl.CostEstimate(flops=flops, bytes_accessed=0, transcendentals=0),
        name=name,
    )


def column_to_row(column):
    n = column.shape[0]
    diagonal = lax.broadcasted_iota(jnp.int32, (n, n), 0) == lax.broadcasted_iota(jnp.int32, (n, n), 1)
    return jnp.sum(jnp.where(diagonal, column, 0.0), axis=0, keepdims=True)


def normalise_body(_, sketches_hbm, labels_hbm, ranks_hbm, out, sketches, labels, ranks, sems):
    pairs = ((sketches_hbm, sketches), (labels_hbm, labels), (ranks_hbm, ranks))
    copies = [pltpu.make_async_copy(source, target, sems.at[i]) for i, (source, target) in enumerate(pairs)]
    for copy in copies:
        copy.start()
    for copy in copies[1:]:
        copy.wait()
    label_row = column_to_row(labels[...].astype(jnp.float32))
    rank_row = ranks[...]
    high = (rank_row // 256).astype(jnp.float32)
    low = (rank_row % 256).astype(jnp.float32)
    index = lax.broadcasted_iota(jnp.int32, (KEYS, ROWS), 0)
    rows = jnp.where(index == 0, label_row, jnp.where(index == 1, high, jnp.where(index == 2, low, 0.0)))
    out[ROWS : ROWS + KEYS, :] = jnp.zeros((KEYS, DIM), jnp.bfloat16)
    out[ROWS : ROWS + KEYS, 0:ROWS] = rows.astype(jnp.bfloat16)
    copies[0].wait()
    values = sketches[...]
    scale = lax.rsqrt(jnp.sum(values * values, axis=1, keepdims=True) + 1e-06)
    out[0:ROWS, :] = (values * scale).astype(jnp.bfloat16)


def count_of(block):
    return block.shape[0] // ROWS


def key_of(rows):
    return rows[0:1] * 65536.0 + rows[1:2] * 256.0 + rows[2:3]


def join_body(*refs):
    out, columns, start = refs[-1], [], 0
    for ref in refs[:-1]:
        size = count_of(ref) * ROWS
        out[start : start + size, :] = ref[0:size, :]
        width = -(-size // 128) * 128
        keys = ref[size : size + KEYS, 0:width].astype(jnp.float32)[0:8]
        columns.append(jnp.transpose(keys)[0:size])
        start += size
    rows = jnp.transpose(jnp.concatenate(columns, axis=0))
    out[start : start + KEYS, :] = jnp.zeros((KEYS, DIM), jnp.bfloat16)
    out[start : start + KEYS, 0:start] = jnp.concatenate([rows, jnp.zeros_like(rows)], axis=0).astype(jnp.bfloat16)


def join(name, *blocks, flops=0):
    total = sum(count_of(b) for b in blocks)
    shape = jax.ShapeDtypeStruct((total * ROWS + KEYS, DIM), jnp.bfloat16)
    return call(join_body, shape, count=len(blocks), flops=flops, name=name)(*blocks)


def highest(first, *rest):
    for rows in rest:
        first = jnp.maximum(first, rows)
    return first


def after_kernel(arrays, token):
    return lax.optimization_barrier((*arrays, token))[:-1]


def score(queries, bundles, name, token=None, weight=1):
    refs, layout = [], []
    for bundle in bundles:
        layout.append(len(bundle))
        refs += bundle
    blocks = [count_of(q) for q in queries]
    total, length = sum(blocks), 4 * ROWS
    halved = 2 in layout

    def body(*args):
        args = list(args)
        joined = args.pop() if halved else None
        if token is not None:
            args.pop(0)
        q_refs, k_refs, out = args[: len(queries)], args[len(queries) : -1], args[-1]
        parts = []
        for n in layout:
            if n == 1:
                whole = k_refs[0]
                key_rows = whole[length : length + KEYS, 0:length]
            else:
                top, bottom = k_refs[:2]
                joined[0 : length // 2, :] = top[0 : length // 2, :]
                joined[length // 2 : length, :] = bottom[0 : length // 2, :]
                whole = joined
                key_rows = bottom[length // 2 : length // 2 + KEYS, 0:length]
            k_refs = k_refs[n:]
            key = key_of(key_rows.astype(jnp.float32)[0:8])
            parts += [(whole, start, key[:, start : start + 256]) for start in range(0, length, 256)]
        row = 0
        for q_ref, count in zip(q_refs, blocks):
            size = count * ROWS
            key_row = key_of(q_ref[size : size + KEYS, 0:size].astype(jnp.float32)[0:8])
            key_q = jnp.transpose(jnp.broadcast_to(key_row, (8, size)))[:, 0:1]
            base = jnp.floor(key_q * (1.0 / 65536.0)) * 65536.0
            best = jnp.full((size, 128), -1.0, jnp.float32)
            for ref, start, key_k in parts:
                scores = lax.dot_general(
                    q_ref[0:size, :], ref[start : start + 256, :], (((1,), (1,)), ((), ())), preferred_element_type=jnp.float32
                )
                allowed = (key_k < key_q) & (key_k >= base)
                scores = jnp.where(allowed, scores, -1.0)
                best = jnp.maximum(best, jnp.maximum(scores[:, 0:128], scores[:, 128:256]))
            top = jnp.max(best, axis=1, keepdims=True)
            for i in range(count):
                out[row : row + 1, :] = column_to_row(top[i * ROWS : (i + 1) * ROWS])
                row += 1

    flops = int(2 * DIM * ROWS * ROWS * total * 4 * len(bundles) * weight * WEIGHT)
    operands = ([] if token is None else [token]) + list(queries) + refs
    return call(
        body,
        jax.ShapeDtypeStruct((total, ROWS), jnp.float32),
        scratch=[pltpu.VMEM((length, DIM), jnp.bfloat16)] if halved else [],
        flops=flops,
        count=len(operands),
        name=name,
    )(*operands)


def on_device(sketches, labels, ranks):
    core = lax.axis_index("core").astype(jnp.int32)
    z = lax.axis_index("z").astype(jnp.int32)
    place = jnp.stack([core, z])
    own = call(
        normalise_body,
        jax.ShapeDtypeStruct((ROWS + KEYS, DIM), jnp.bfloat16),
        scratch=[
            pltpu.VMEM((ROWS, DIM), jnp.float32),
            pltpu.VMEM((ROWS, 1), jnp.int32),
            pltpu.VMEM((1, ROWS), jnp.int32),
            pltpu.SemaphoreType.DMA((3,)),
        ],
        spaces=[SMEM] + [HBM] * 3,
        name="normalise",
    )(place, sketches, labels, ranks.reshape(1, ROWS))

    def first(step):
        return lambda x, c, z, y: (x + step * (1 - c), c, z, y + step * c)

    def second(step):
        return lambda x, c, z, y: (x + step * c, c, z, y + step * (1 - c))

    def along_z(x, c, z, y):
        return (x, c, z + 1 - 2 * c, y)

    def across(x, c, z, y):
        return (x, c + 1, z, y)

    half = 2 * ROWS
    partner = send(own, across, "partner")
    line = [send(own, first(2), "key_far"), send(own, first(1), "key_up"), send(own, first(-1), "key_down")]
    here = join("here", own, partner, flops=4 << 30)
    r1 = send(here, along_z, "r1")
    bundle = join("bundle", own, *line)
    after, before = send(bundle, second(-1), "bundle_down"), send(bundle, second(1), "bundle_up")
    s0 = score([here], [[bundle]], "s0", weight=10)
    (r1,) = after_kernel([r1], s0)
    r2, e1 = send(r1, along_z, "r2"), send(r1, across, "e1")
    s1 = score([r1, e1], [[bundle]], "s1")
    (r2,) = after_kernel([r2], s1)
    r3, e2 = send(r2, along_z, "r3"), send(r2, across, "e2")
    after, before, r2 = after_kernel([after, before, r2], r2)
    opposite = [send(before[0 : half + KEYS], second(1), "opposite_up"), send(after[half:], second(-1), "opposite_down")]
    s2 = score([here, r1, e1], [[after], [before]], "s2")
    (r3,) = after_kernel([r3], s2)
    r4, e3 = send(r3, along_z, "r4"), send(r3, across, "e3")
    s3 = score([r2, e2], [[bundle], [after], [before]], "s3", r3)
    opposite = after_kernel(opposite, s3)
    s4 = score([r3, e3], [[bundle], [after], [before], opposite], "s4")
    s5 = score([here, r1, e1, r2, e2], [opposite], "s5", s4)
    (r4,) = after_kernel([r4], s5)
    s6 = score([r4], [[bundle], [after], [before], opposite], "s6")

    def merge_body(at, s0, s1, s2, s3, s4, s5, s6, out):
        me, level = at[0], at[1]
        sign = 2 * me - 1
        two, five = s2[...], s5[...]
        groups = (
            highest(s0[...], two[0:2], five[0:2]),
            highest(s1[...], two[2:6], five[2:6]),
            highest(s3[...], five[6:10]),
            s4[...],
            s6[...],
        )
        for k, rows in enumerate(groups):
            for j in range(rows.shape[0]):
                which = me if j in (0, 3) else 1 - me
                step = k if k in (0, 4) else (sign * k if j < 2 else -sign * k)
                out[pl.ds(which * 8 + lax.rem(level + step + 16, 8), 1), :] = rows[j : j + 1]

    scores = (s0, s1, s2, s3, s4, s5, s6)
    partial = call(
        merge_body, jax.ShapeDtypeStruct((16, ROWS), jnp.float32), spaces=[SMEM] + [VMEM] * len(scores), name="merge"
    )(place, *scores)
    returned = lax.all_to_all(partial, ("core", "z"), split_axis=0, concat_axis=0, tiled=True)
    return jnp.max(returned, axis=0)


def solution(mesh):
    fine = Mesh(mesh.devices.reshape(SIZES), AXES)
    return jax.shard_map(
        on_device,
        mesh=fine,
        in_specs=(P(AXES, None), P(AXES, None), P(AXES)),
        out_specs=P(AXES),
        check_vma=False,
    )
```

```python
import jax
import jax.numpy as jnp
import numpy as np
from jax import lax
from jax.experimental import pallas as pl
from jax.experimental.pallas import tpu as pltpu
from jax.sharding import Mesh, PartitionSpec as P

AXES = ("x", "core", "z", "y")
SIZES = (4, 2, 8, 4)
ROWS = 192
WEIGHT = 1
W2, W3, W5, W6, W7 = 10, 10, 1, 1, 10
KEYS = 16
DIM = 1024
VMEM = pl.BlockSpec(memory_space=pltpu.VMEM)
SMEM = pl.BlockSpec(memory_space=pltpu.SMEM)


def permutation(move):
    pairs = []
    for source in np.ndindex(*SIZES):
        target = np.array(move(*source)) % np.array(SIZES)
        pairs.append((int(np.ravel_multi_index(source, SIZES)), int(np.ravel_multi_index(tuple(target), SIZES))))
    return pairs


def send(array, move, name):
    with jax.named_scope(name):
        return lax.ppermute(array, AXES, permutation(move))


def call(body, outs, scratch=(), flops=0, spaces=None, count=0, name=None, vmem=16):
    return pl.pallas_call(
        body,
        out_shape=outs,
        in_specs=spaces or [VMEM] * count,
        out_specs=VMEM if isinstance(outs, jax.ShapeDtypeStruct) else [VMEM] * len(outs),
        scratch_shapes=list(scratch),
        compiler_params=pltpu.CompilerParams(vmem_limit_bytes=vmem << 20),
        cost_estimate=pl.CostEstimate(flops=flops, bytes_accessed=0, transcendentals=0),
        name=name,
    )


def column_to_row(column):
    n = column.shape[0]
    diagonal = lax.broadcasted_iota(jnp.int32, (n, n), 0) == lax.broadcasted_iota(jnp.int32, (n, n), 1)
    return jnp.sum(jnp.where(diagonal, column, 0.0), axis=0, keepdims=True)


def normalise_body(_, sketches, labels, ranks, out):
    rank_row = ranks[...]
    high = (rank_row // 256).astype(jnp.float32)
    low = (rank_row % 256).astype(jnp.float32)
    index = lax.broadcasted_iota(jnp.int32, (KEYS, ROWS), 0)
    rows = jnp.where(index == 0, labels[...].astype(jnp.float32), jnp.where(index == 1, high, jnp.where(index == 2, low, 0.0)))
    out[ROWS : ROWS + KEYS, :] = jnp.zeros((KEYS, DIM), jnp.bfloat16)
    out[ROWS : ROWS + KEYS, 0:ROWS] = rows.astype(jnp.bfloat16)
    values = sketches[...]
    scale = lax.rsqrt(jnp.sum(values * values, axis=1, keepdims=True) + 1e-06)
    out[0:ROWS, :] = (values * scale).astype(jnp.bfloat16)


def count_of(block):
    return block.shape[0] // ROWS


def key_of(rows):
    return rows[0:1] * 65536.0 + rows[1:2] * 256.0 + rows[2:3]


def join_body(*refs):
    out, columns, start = refs[-1], [], 0
    for ref in refs[:-1]:
        size = count_of(ref) * ROWS
        out[start : start + size, :] = ref[0:size, :]
        width = -(-size // 128) * 128
        keys = ref[size : size + KEYS, 0:width].astype(jnp.float32)[0:8]
        columns.append(jnp.transpose(keys)[0:size])
        start += size
    rows = jnp.transpose(jnp.concatenate(columns, axis=0))
    out[start : start + KEYS, :] = jnp.zeros((KEYS, DIM), jnp.bfloat16)
    out[start : start + KEYS, 0:start] = jnp.concatenate([rows, jnp.zeros_like(rows)], axis=0).astype(jnp.bfloat16)


def join(name, *blocks, flops=0):
    total = sum(count_of(b) for b in blocks)
    shape = jax.ShapeDtypeStruct((total * ROWS + KEYS, DIM), jnp.bfloat16)
    return call(join_body, shape, count=len(blocks), flops=flops, name=name)(*blocks)


def highest(first, *rest):
    for rows in rest:
        first = jnp.maximum(first, rows)
    return first


def after_kernel(arrays, token):
    return lax.optimization_barrier((*arrays, token))[:-1]


def score(tasks, name, token=None, weight=1):
    arrays = []

    def place_of(array):
        for i, known in enumerate(arrays):
            if known is array:
                return i
        arrays.append(array)
        return len(arrays) - 1

    plan = [(place_of(query), count_of(query), [tuple(map(place_of, bundle)) for bundle in bundles]) for query, bundles in tasks]
    pairs = list(dict.fromkeys(pair for _, _, bundles in plan for pair in bundles))
    total, half = sum(count for _, count, _ in plan), 2 * ROWS

    def body(*args):
        refs, out, joined = args[: len(arrays)], args[-2], args[-1]
        parts = {}
        for i, (top, bottom) in enumerate(pairs):
            top, bottom = refs[top], refs[bottom]
            joined[i, 0:128, :] = top[256:half, :]
            joined[i, 128:256, :] = bottom[0:128, :]
            rows = [key_of(ref[half : half + KEYS, 0:half].astype(jnp.float32)[0:8]) for ref in (top, bottom)]
            key = jnp.concatenate(rows, axis=1)
            tiles = (lambda t=top: t[0:256, :], lambda i=i: joined[i], lambda b=bottom: b[128:half, :])
            parts[pairs[i]] = [(tile, key[:, 256 * j : 256 * j + 256]) for j, tile in enumerate(tiles)]
        row = 0
        for at, count, bundles in plan:
            q_ref, size = refs[at], count * ROWS
            width = -(-size // 128) * 128
            key_row = key_of(q_ref[size : size + KEYS, 0:width].astype(jnp.float32)[0:8])
            key_q = jnp.transpose(jnp.broadcast_to(key_row, (8, width)))[0:size, 0:1]
            base = jnp.floor(key_q * (1.0 / 65536.0)) * 65536.0
            best = jnp.full((size, 128), -1.0, jnp.float32)
            for bundle in bundles:
                for tile, key_k in parts[bundle]:
                    scores = lax.dot_general(
                        q_ref[0:size, :], tile(), (((1,), (1,)), ((), ())), preferred_element_type=jnp.float32
                    )
                    allowed = (key_k < key_q) & (key_k >= base)
                    scores = jnp.where(allowed, scores, -1.0)
                    best = jnp.maximum(best, jnp.maximum(scores[:, 0:128], scores[:, 128:256]))
            top = jnp.max(best, axis=1, keepdims=True)
            for i in range(count):
                out[row : row + 1, :] = column_to_row(top[i * ROWS : (i + 1) * ROWS])
                row += 1

    flops = sum(2 * DIM * ROWS * ROWS * count * 4 * len(bundles) for _, count, bundles in plan)
    operands = arrays if token is None else arrays + [token]
    return call(
        body,
        jax.ShapeDtypeStruct((total, ROWS), jnp.float32),
        scratch=[pltpu.VMEM((len(pairs), 256, DIM), jnp.bfloat16)],
        flops=int(flops * weight),
        count=len(operands),
        name=name,
    )(*operands)


def on_device(sketches, labels, ranks):
    core = lax.axis_index("core").astype(jnp.int32)
    z = lax.axis_index("z").astype(jnp.int32)
    place = jnp.stack([core, z])
    single = jax.ShapeDtypeStruct((ROWS + KEYS, DIM), jnp.bfloat16)
    own = call(normalise_body, single, spaces=[SMEM] + [VMEM] * 3, name="normalise")(
        place, sketches, labels.reshape(1, ROWS), ranks.reshape(1, ROWS)
    )

    def first(step):
        return lambda x, c, z, y: (x + step * (1 - c), c, z, y + step * c)

    def second(step):
        return lambda x, c, z, y: (x + step * c, c, z, y + step * (1 - c))

    def along_z(x, c, z, y):
        return (x, c, z + 1 - 2 * c, y)

    def across(x, c, z, y):
        return (x, c + 1, z, y)

    partner = send(own, across, "partner")
    key_far, key_up, key_down = send(own, first(2), "key_far"), send(own, first(1), "key_up"), send(own, first(-1), "key_down")
    here = join("here", own, partner, flops=4 << 30)
    r1 = send(here, along_z, "r1")
    ka = join("ka", own, key_down)
    after_a, before_a = send(ka, second(-1), "ka_down"), send(ka, second(1), "ka_up")
    key_far, key_up = after_kernel([key_far, key_up], ka)
    kb = join("kb", key_up, key_far)
    base = [(ka, kb)]
    s0 = score([(here, base)], "s0", weight=10)
    (r1,) = after_kernel([r1], s0)
    r2, e1 = send(r1, along_z, "r2"), send(r1, across, "e1")
    s1 = score([(r1, base)], "s1", weight=10)
    after_a, before_a, e1 = after_kernel([after_a, before_a, e1], s1)
    (kb_later,) = after_kernel([kb], before_a)
    after_b, before_b = send(kb_later, second(-1), "kb_down"), send(kb_later, second(1), "kb_up")
    opposite_a = send(before_a, second(1), "opposite_a")
    near_a = [(after_a, before_a)]
    s2 = score([(here, near_a), (r1, near_a), (e1, base + near_a)], "s2", weight=W2)
    (r2,) = after_kernel([r2], s2)
    r3, e2 = send(r2, along_z, "r3"), send(r2, across, "e2")
    s3 = score([(r2, base + near_a)], "s3", weight=W3)
    (e2,) = after_kernel([e2], s3)
    s4 = score([(e2, base + near_a)], "s4", weight=W3)
    after_b, before_b = after_kernel([after_b, before_b], s4)
    opposite_b = send(after_b, second(-1), "opposite_b")
    near_b = [(after_b, before_b)]
    s5 = score([(q, near_b) for q in (here, r1, e1, r2, e2)], "s5", weight=W5)
    (r3,) = after_kernel([r3], s5)
    r4, e3 = send(r3, along_z, "r4"), send(r3, across, "e3")
    s7 = score([(r3, base + near_a + near_b)], "s7", weight=W7)
    (e3,) = after_kernel([e3], s7)
    s6 = score([(e3, base + near_a + near_b)], "s6", weight=W6)
    opposite_a, opposite_b = after_kernel([opposite_a, opposite_b], s6)
    opposite = [(opposite_a, opposite_b)]
    s8 = score([(q, opposite) for q in (here, r1, e1, r2, e2, r3, e3)], "s8")
    (r4,) = after_kernel([r4], s8)
    s9 = score([(r4, base + near_a + near_b + opposite)], "s9")

    def merge_body(at, s0, s1, s2, s3, s4, s5, s6, s7, s8, s9, out):
        me, level = at[0], at[1]
        sign = 2 * me - 1
        two, five, eight = s2[...], s5[...], s8[...]
        groups = (
            (highest(s0[...], two[0:2], five[0:2], eight[0:2]), 0),
            (highest(s1[...], two[2:4], five[2:4], eight[2:4]), sign),
            (highest(two[4:6], five[4:6], eight[4:6]), -sign),
            (highest(s3[...], five[6:8], eight[6:8]), 2 * sign),
            (highest(s4[...], five[8:10], eight[8:10]), -2 * sign),
            (highest(s7[...], eight[10:12]), 3 * sign),
            (highest(s6[...], eight[12:14]), -3 * sign),
            (s9[...], 4),
        )
        for k, (rows, step) in enumerate(groups):
            for j in range(2):
                which = me if (j == 0) != (k in (2, 4, 6)) else 1 - me
                out[pl.ds(which * 8 + lax.rem(level + step + 16, 8), 1), :] = rows[j : j + 1]

    scores = (s0, s1, s2, s3, s4, s5, s6, s7, s8, s9)
    partial = call(
        merge_body, jax.ShapeDtypeStruct((16, ROWS), jnp.float32), spaces=[SMEM] + [VMEM] * len(scores), name="merge"
    )(place, *scores)
    returned = lax.all_to_all(partial, ("core", "z"), split_axis=0, concat_axis=0, tiled=True)
    return jnp.max(returned, axis=0)


def solution(mesh):
    fine = Mesh(mesh.devices.reshape(SIZES), AXES)
    return jax.shard_map(
        on_device,
        mesh=fine,
        in_specs=(P(AXES, None), P(AXES, None), P(AXES)),
        out_specs=P(AXES),
        check_vma=False,
    )
```

```python
import jax
import jax.numpy as jnp
import numpy as np
from jax import lax
from jax.experimental import pallas as pl
from jax.experimental.pallas import tpu as pltpu
from jax.sharding import Mesh, PartitionSpec as P

AXES = ("x", "core", "z", "y")
SIZES = (4, 2, 8, 4)
ROWS = 192
WEIGHT = 1
W2, W3, W5, W6, W7 = 10, 10, 1, 1, 10
KEYS = 16
DIM = 1024
VMEM = pl.BlockSpec(memory_space=pltpu.VMEM)


def permutation(move):
    pairs = []
    for source in np.ndindex(*SIZES):
        target = np.array(move(*source)) % np.array(SIZES)
        pairs.append((int(np.ravel_multi_index(source, SIZES)), int(np.ravel_multi_index(tuple(target), SIZES))))
    return pairs


def send(array, move, name):
    with jax.named_scope(name):
        return lax.ppermute(array, AXES, permutation(move))


def call(body, outs, scratch=(), flops=0, spaces=None, count=0, name=None, vmem=16):
    return pl.pallas_call(
        body,
        out_shape=outs,
        in_specs=spaces or [VMEM] * count,
        out_specs=VMEM if isinstance(outs, jax.ShapeDtypeStruct) else [VMEM] * len(outs),
        scratch_shapes=list(scratch),
        compiler_params=pltpu.CompilerParams(vmem_limit_bytes=vmem << 20),
        cost_estimate=pl.CostEstimate(flops=flops, bytes_accessed=0, transcendentals=0),
        name=name,
    )


def column_to_row(column):
    n = column.shape[0]
    diagonal = lax.broadcasted_iota(jnp.int32, (n, n), 0) == lax.broadcasted_iota(jnp.int32, (n, n), 1)
    return jnp.sum(jnp.where(diagonal, column, 0.0), axis=0, keepdims=True)


def normalise_body(sketches, labels, ranks, out):
    rank_row = ranks[...]
    high = (rank_row // 256).astype(jnp.float32)
    low = (rank_row % 256).astype(jnp.float32)
    index = lax.broadcasted_iota(jnp.int32, (KEYS, ROWS), 0)
    rows = jnp.where(index == 0, labels[...].astype(jnp.float32), jnp.where(index == 1, high, jnp.where(index == 2, low, 0.0)))
    out[ROWS : ROWS + KEYS, :] = jnp.zeros((KEYS, DIM), jnp.bfloat16)
    out[ROWS : ROWS + KEYS, 0:ROWS] = rows.astype(jnp.bfloat16)
    values = sketches[...]
    scale = lax.rsqrt(jnp.sum(values * values, axis=1, keepdims=True) + 1e-06)
    out[0:ROWS, :] = (values * scale).astype(jnp.bfloat16)


def count_of(block):
    return block.shape[0] // ROWS


def key_of(rows):
    return rows[0:1] * 65536.0 + rows[1:2] * 256.0 + rows[2:3]


def join_body(*refs):
    out, columns, start = refs[-1], [], 0
    for ref in refs[:-1]:
        size = count_of(ref) * ROWS
        out[start : start + size, :] = ref[0:size, :]
        width = -(-size // 128) * 128
        keys = ref[size : size + KEYS, 0:width].astype(jnp.float32)[0:8]
        columns.append(jnp.transpose(keys)[0:size])
        start += size
    rows = jnp.transpose(jnp.concatenate(columns, axis=0))
    out[start : start + KEYS, :] = jnp.zeros((KEYS, DIM), jnp.bfloat16)
    out[start : start + KEYS, 0:start] = jnp.concatenate([rows, jnp.zeros_like(rows)], axis=0).astype(jnp.bfloat16)


def join(name, *blocks, flops=0):
    total = sum(count_of(b) for b in blocks)
    shape = jax.ShapeDtypeStruct((total * ROWS + KEYS, DIM), jnp.bfloat16)
    return call(join_body, shape, count=len(blocks), flops=flops, name=name)(*blocks)


def highest(first, *rest):
    for rows in rest:
        first = jnp.maximum(first, rows)
    return first


def after_kernel(arrays, token):
    return lax.optimization_barrier((*arrays, token))[:-1]


def score(tasks, name, token=None, weight=1, extra=(), finish=None):
    arrays = []

    def place_of(array):
        for i, known in enumerate(arrays):
            if known is array:
                return i
        arrays.append(array)
        return len(arrays) - 1

    plan = [(place_of(query), count_of(query), [tuple(map(place_of, bundle)) for bundle in bundles]) for query, bundles in tasks]
    pairs = list(dict.fromkeys(pair for _, _, bundles in plan for pair in bundles))
    total, half = sum(count for _, count, _ in plan), 2 * ROWS

    def body(*args):
        refs, out, joined = args[: len(arrays)], args[-2], args[-1]
        found = []
        parts = {}
        for i, (top, bottom) in enumerate(pairs):
            top, bottom = refs[top], refs[bottom]
            joined[i, 0:128, :] = top[256:half, :]
            joined[i, 128:256, :] = bottom[0:128, :]
            rows = [key_of(ref[half : half + KEYS, 0:half].astype(jnp.float32)[0:8]) for ref in (top, bottom)]
            key = jnp.concatenate(rows, axis=1)
            tiles = (lambda t=top: t[0:256, :], lambda i=i: joined[i], lambda b=bottom: b[128:half, :])
            parts[pairs[i]] = [(tile, key[:, 256 * j : 256 * j + 256]) for j, tile in enumerate(tiles)]
        for at, count, bundles in plan:
            q_ref, size = refs[at], count * ROWS
            width = -(-size // 128) * 128
            key_row = key_of(q_ref[size : size + KEYS, 0:width].astype(jnp.float32)[0:8])
            key_q = jnp.transpose(jnp.broadcast_to(key_row, (8, width)))[0:size, 0:1]
            base = jnp.floor(key_q * (1.0 / 65536.0)) * 65536.0
            best = jnp.full((size, 128), -1.0, jnp.float32)
            for bundle in bundles:
                for tile, key_k in parts[bundle]:
                    scores = lax.dot_general(
                        q_ref[0:size, :], tile(), (((1,), (1,)), ((), ())), preferred_element_type=jnp.float32
                    )
                    allowed = (key_k < key_q) & (key_k >= base)
                    scores = jnp.where(allowed, scores, -1.0)
                    best = jnp.maximum(best, jnp.maximum(scores[:, 0:128], scores[:, 128:256]))
            top = jnp.max(best, axis=1, keepdims=True)
            for i in range(count):
                found.append(column_to_row(top[i * ROWS : (i + 1) * ROWS]))
        if finish is None:
            for i, rows in enumerate(found):
                out[i : i + 1, :] = rows
        else:
            finish(*args[len(arrays) : len(arrays) + len(extra)], jnp.concatenate(found, axis=0), out)

    flops = sum(2 * DIM * ROWS * ROWS * count * 4 * len(bundles) for _, count, bundles in plan)
    operands = arrays + list(extra) + ([] if token is None else [token])
    return call(
        body,
        jax.ShapeDtypeStruct((total if finish is None else 16, ROWS), jnp.float32),
        scratch=[pltpu.VMEM((len(pairs), 256, DIM), jnp.bfloat16)],
        flops=int(flops * weight),
        count=len(operands),
        name=name,
    )(*operands)


def on_device(sketches, labels, ranks):
    single = jax.ShapeDtypeStruct((ROWS + KEYS, DIM), jnp.bfloat16)
    own = call(normalise_body, single, count=3, name="normalise")(
        sketches, labels.reshape(1, ROWS), ranks.reshape(1, ROWS)
    )

    def first(step):
        return lambda x, c, z, y: (x + step * (1 - c), c, z, y + step * c)

    def second(step):
        return lambda x, c, z, y: (x + step * c, c, z, y + step * (1 - c))

    def along_z(x, c, z, y):
        return (x, c, z + 1 - 2 * c, y)

    def across(x, c, z, y):
        return (x, c + 1, z, y)

    partner = send(own, across, "partner")
    key_far, key_up, key_down = send(own, first(2), "key_far"), send(own, first(1), "key_up"), send(own, first(-1), "key_down")
    here = join("here", own, partner, flops=4 << 30)
    r1 = send(here, along_z, "r1")
    ka = join("ka", own, key_down)
    after_a, before_a = send(ka, second(-1), "ka_down"), send(ka, second(1), "ka_up")
    key_far, key_up = after_kernel([key_far, key_up], ka)
    kb = join("kb", key_up, key_far)
    base = [(ka, kb)]
    s0 = score([(here, base)], "s0", weight=10)
    (r1,) = after_kernel([r1], s0)
    r2, e1 = send(r1, along_z, "r2"), send(r1, across, "e1")
    s1 = score([(r1, base)], "s1", weight=10)
    after_a, before_a, e1 = after_kernel([after_a, before_a, e1], s1)
    (kb_later,) = after_kernel([kb], before_a)
    after_b, before_b = send(kb_later, second(-1), "kb_down"), send(kb_later, second(1), "kb_up")
    opposite_a = send(before_a, second(1), "opposite_a")
    near_a = [(after_a, before_a)]
    s2 = score([(here, near_a), (r1, near_a), (e1, base + near_a)], "s2", weight=W2)
    (r2,) = after_kernel([r2], s2)
    r3, e2 = send(r2, along_z, "r3"), send(r2, across, "e2")
    s3 = score([(r2, base + near_a)], "s3", weight=W3)
    (e2,) = after_kernel([e2], s3)
    s4 = score([(e2, base + near_a)], "s4", weight=W3)
    after_b, before_b = after_kernel([after_b, before_b], s4)
    opposite_b = send(after_b, second(-1), "opposite_b")
    near_b = [(after_b, before_b)]
    s5 = score([(q, near_b) for q in (here, r1, e1, r2, e2)], "s5", weight=W5)
    (r3,) = after_kernel([r3], s5)
    r4, e3 = send(r3, along_z, "r4"), send(r3, across, "e3")
    s7 = score([(r3, base + near_a + near_b)], "s7", weight=W7)
    (e3,) = after_kernel([e3], s7)
    s6 = score([(e3, base + near_a + near_b)], "s6", weight=W6)
    opposite_a, opposite_b = after_kernel([opposite_a, opposite_b], s6)
    opposite = [(opposite_a, opposite_b)]
    s8 = score([(q, opposite) for q in (here, r1, e1, r2, e2, r3, e3)], "s8")
    (r4,) = after_kernel([r4], s8)
    def merge_body(s0, s1, s2, s3, s4, s5, s6, s7, s8, s9, out):
        me, level = lax.axis_index("core"), lax.axis_index("z")
        sign = 2 * me - 1
        two, five, eight = s2[...], s5[...], s8[...]
        groups = (
            (highest(s0[...], two[0:2], five[0:2], eight[0:2]), 0),
            (highest(s1[...], two[2:4], five[2:4], eight[2:4]), sign),
            (highest(two[4:6], five[4:6], eight[4:6]), -sign),
            (highest(s3[...], five[6:8], eight[6:8]), 2 * sign),
            (highest(s4[...], five[8:10], eight[8:10]), -2 * sign),
            (highest(s7[...], eight[10:12]), 3 * sign),
            (highest(s6[...], eight[12:14]), -3 * sign),
            (s9, 4),
        )
        for k, (rows, step) in enumerate(groups):
            for j in range(2):
                which = me if (j == 0) != (k in (2, 4, 6)) else 1 - me
                out[pl.ds(which * 8 + lax.rem(level + step + 16, 8), 1), :] = rows[j : j + 1]

    scores = (s0, s1, s2, s3, s4, s5, s6, s7, s8)
    partial = score([(r4, base + near_a + near_b + opposite)], "s9", extra=scores, finish=merge_body)
    returned = lax.all_to_all(partial, ("core", "z"), split_axis=0, concat_axis=0, tiled=True)
    return jnp.max(returned, axis=0)


def solution(mesh):
    fine = Mesh(mesh.devices.reshape(SIZES), AXES)
    return jax.shard_map(
        on_device,
        mesh=fine,
        in_specs=(P(AXES, None), P(AXES, None), P(AXES)),
        out_specs=P(AXES),
        check_vma=False,
    )
```

```python
import jax
import jax.numpy as jnp
import numpy as np
from jax import lax
from jax.experimental import pallas as pl
from jax.experimental.pallas import tpu as pltpu
from jax.sharding import Mesh, PartitionSpec as P

AXES = ("x", "core", "z", "y")
SIZES = (4, 2, 8, 4)
ROWS = 192
WEIGHT = 1
W2, W3, W5, W6, W7 = 10, 10, 1, 1, 10
KEYS = 16
DIM = 1024
VMEM = pl.BlockSpec(memory_space=pltpu.VMEM)


def permutation(move):
    pairs = []
    for source in np.ndindex(*SIZES):
        target = np.array(move(*source)) % np.array(SIZES)
        pairs.append((int(np.ravel_multi_index(source, SIZES)), int(np.ravel_multi_index(tuple(target), SIZES))))
    return pairs


def send(array, move, name):
    with jax.named_scope(name):
        return lax.ppermute(array, AXES, permutation(move))


def call(body, outs, scratch=(), flops=0, spaces=None, count=0, name=None, vmem=16):
    return pl.pallas_call(
        body,
        out_shape=outs,
        in_specs=spaces or [VMEM] * count,
        out_specs=VMEM if isinstance(outs, jax.ShapeDtypeStruct) else [VMEM] * len(outs),
        scratch_shapes=list(scratch),
        compiler_params=pltpu.CompilerParams(vmem_limit_bytes=vmem << 20),
        cost_estimate=pl.CostEstimate(flops=flops, bytes_accessed=0, transcendentals=0),
        name=name,
    )


def column_to_row(column):
    n = column.shape[0]
    diagonal = lax.broadcasted_iota(jnp.int32, (n, n), 0) == lax.broadcasted_iota(jnp.int32, (n, n), 1)
    return jnp.sum(jnp.where(diagonal, column, 0.0), axis=0, keepdims=True)


def normalise_body(sketches, labels, ranks, out):
    rank_row = ranks[...]
    high = (rank_row // 256).astype(jnp.float32)
    low = (rank_row % 256).astype(jnp.float32)
    index = lax.broadcasted_iota(jnp.int32, (KEYS, ROWS), 0)
    rows = jnp.where(index == 0, labels[...].astype(jnp.float32), jnp.where(index == 1, high, jnp.where(index == 2, low, 0.0)))
    out[ROWS : ROWS + KEYS, :] = jnp.zeros((KEYS, DIM), jnp.bfloat16)
    out[ROWS : ROWS + KEYS, 0:ROWS] = rows.astype(jnp.bfloat16)
    values = sketches[...]
    scale = lax.rsqrt(jnp.sum(values * values, axis=1, keepdims=True) + 1e-06)
    out[0:ROWS, :] = (values * scale).astype(jnp.bfloat16)


def count_of(block):
    return block.shape[0] // ROWS


def key_of(rows):
    return rows[0:1] * 65536.0 + rows[1:2] * 256.0 + rows[2:3]


def join_body(*refs):
    out, columns, start = refs[-1], [], 0
    for ref in refs[:-1]:
        size = count_of(ref) * ROWS
        out[start : start + size, :] = ref[0:size, :]
        width = -(-size // 128) * 128
        keys = ref[size : size + KEYS, 0:width].astype(jnp.float32)[0:8]
        columns.append(jnp.transpose(keys)[0:size])
        start += size
    rows = jnp.transpose(jnp.concatenate(columns, axis=0))
    out[start : start + KEYS, :] = jnp.zeros((KEYS, DIM), jnp.bfloat16)
    out[start : start + KEYS, 0:start] = jnp.concatenate([rows, jnp.zeros_like(rows)], axis=0).astype(jnp.bfloat16)


def join(name, *blocks, flops=0):
    total = sum(count_of(b) for b in blocks)
    shape = jax.ShapeDtypeStruct((total * ROWS + KEYS, DIM), jnp.bfloat16)
    return call(join_body, shape, count=len(blocks), flops=flops, name=name)(*blocks)


def highest(first, *rest):
    for rows in rest:
        first = jnp.maximum(first, rows)
    return first


def after_kernel(arrays, token):
    return lax.optimization_barrier((*arrays, token))[:-1]


def score(tasks, name, token=None, weight=1, extra=(), finish=None):
    arrays = []

    def place_of(array):
        for i, known in enumerate(arrays):
            if known is array:
                return i
        arrays.append(array)
        return len(arrays) - 1

    plan = [(place_of(query), count_of(query), [tuple(map(place_of, bundle)) for bundle in bundles]) for query, bundles in tasks]
    pairs = list(dict.fromkeys(pair for _, _, bundles in plan for pair in bundles))
    total, half = sum(count for _, count, _ in plan), 2 * ROWS

    def body(*args):
        refs, out, joined = args[: len(arrays)], args[-2], args[-1]
        found = []
        parts = {}
        for i, (top, bottom) in enumerate(pairs):
            top, bottom = refs[top], refs[bottom]
            joined[i, 0:128, :] = top[256:half, :]
            joined[i, 128:256, :] = bottom[0:128, :]
            rows = [key_of(ref[half : half + KEYS, 0:half].astype(jnp.float32)[0:8]) for ref in (top, bottom)]
            key = jnp.concatenate(rows, axis=1)
            tiles = (lambda t=top: t[0:256, :], lambda i=i: joined[i], lambda b=bottom: b[128:half, :])
            parts[pairs[i]] = [(tile, key[:, 256 * j : 256 * j + 256]) for j, tile in enumerate(tiles)]
        for at, count, bundles in plan:
            q_ref, size = refs[at], count * ROWS
            width = -(-size // 128) * 128
            key_row = key_of(q_ref[size : size + KEYS, 0:width].astype(jnp.float32)[0:8])
            key_q = jnp.transpose(jnp.broadcast_to(key_row, (8, width)))[0:size, 0:1]
            base = jnp.floor(key_q * (1.0 / 65536.0)) * 65536.0
            best = jnp.full((size, 128), -1.0, jnp.float32)
            for bundle in bundles:
                for tile, key_k in parts[bundle]:
                    scores = lax.dot_general(
                        q_ref[0:size, :], tile(), (((1,), (1,)), ((), ())), preferred_element_type=jnp.float32
                    )
                    allowed = (key_k < key_q) & (key_k >= base)
                    scores = jnp.where(allowed, scores, -1.0)
                    best = jnp.maximum(best, jnp.maximum(scores[:, 0:128], scores[:, 128:256]))
            top = jnp.max(best, axis=1, keepdims=True)
            for i in range(count):
                found.append(column_to_row(top[i * ROWS : (i + 1) * ROWS]))
        if finish is None:
            for i, rows in enumerate(found):
                out[i : i + 1, :] = rows
        else:
            finish(*args[len(arrays) : len(arrays) + len(extra)], jnp.concatenate(found, axis=0), out)

    flops = sum(2 * DIM * ROWS * ROWS * count * 4 * len(bundles) for _, count, bundles in plan)
    operands = arrays + list(extra) + ([] if token is None else [token])
    return call(
        body,
        jax.ShapeDtypeStruct((total if finish is None else 16, ROWS), jnp.float32),
        scratch=[pltpu.VMEM((len(pairs), 256, DIM), jnp.bfloat16)],
        flops=int(flops * weight),
        count=len(operands),
        name=name,
    )(*operands)


def on_device(sketches, labels, ranks):
    single = jax.ShapeDtypeStruct((ROWS + KEYS, DIM), jnp.bfloat16)
    own = call(normalise_body, single, count=3, name="normalise")(
        sketches, labels.reshape(1, ROWS), ranks.reshape(1, ROWS)
    )

    def first(step):
        return lambda x, c, z, y: (x + step * (1 - c), c, z, y + step * c)

    def second(step):
        return lambda x, c, z, y: (x + step * c, c, z, y + step * (1 - c))

    def along_z(x, c, z, y):
        return (x, c, z + 1 - 2 * c, y)

    def across(x, c, z, y):
        return (x, c + 1, z, y)

    partner = send(own, across, "partner")
    key_far, key_up, key_down = send(own, first(2), "key_far"), send(own, first(1), "key_up"), send(own, first(-1), "key_down")
    here = join("here", own, partner, flops=4 << 30)
    r1 = send(here, along_z, "r1")
    ka = join("ka", own, key_down)
    after_a, before_a = send(ka, second(-1), "ka_down"), send(ka, second(1), "ka_up")
    key_far, key_up = after_kernel([key_far, key_up], ka)
    kb = join("kb", key_up, key_far)
    base = [(ka, kb)]
    s0 = score([(here, base)], "s0", weight=10)
    (r1,) = after_kernel([r1], s0)
    r2, e1 = send(r1, along_z, "r2"), send(r1, across, "e1")
    s1 = score([(r1, base)], "s1", weight=10)
    after_a, before_a, e1 = after_kernel([after_a, before_a, e1], s1)
    (kb_later,) = after_kernel([kb], before_a)
    after_b, before_b = send(kb_later, second(-1), "kb_down"), send(kb_later, second(1), "kb_up")
    near_a = [(after_a, before_a)]
    s2 = score([(here, near_a), (r1, near_a), (e1, base + near_a)], "s2", weight=W2)
    (r2,) = after_kernel([r2], s2)
    r3, e2 = send(r2, along_z, "r3"), send(r2, across, "e2")
    s3 = score([(r2, base + near_a)], "s3", weight=W3)
    (before_a_later,) = after_kernel([before_a], s3)
    opposite_a = send(before_a_later, second(1), "opposite_a")
    (e2,) = after_kernel([e2], s3)
    s4 = score([(e2, base + near_a)], "s4", weight=W3)
    after_b, before_b = after_kernel([after_b, before_b], s4)
    opposite_b = send(after_b, second(-1), "opposite_b")
    near_b = [(after_b, before_b)]
    s5 = score([(q, near_b) for q in (here, r1, e1, r2, e2)], "s5", weight=W5)
    (r3,) = after_kernel([r3], s5)
    r4, e3 = send(r3, along_z, "r4"), send(r3, across, "e3")
    s7 = score([(r3, base + near_a + near_b)], "s7", weight=W7)
    (e3,) = after_kernel([e3], s7)
    s6 = score([(e3, base + near_a + near_b)], "s6", weight=W6)
    opposite_a, opposite_b = after_kernel([opposite_a, opposite_b], s6)
    opposite = [(opposite_a, opposite_b)]
    s8 = score([(q, opposite) for q in (here, r1, e1, r2, e2, r3, e3)], "s8")
    (r4,) = after_kernel([r4], s8)
    def merge_body(s0, s1, s2, s3, s4, s5, s6, s7, s8, s9, out):
        me, level = lax.axis_index("core"), lax.axis_index("z")
        sign = 2 * me - 1
        two, five, eight = s2[...], s5[...], s8[...]
        groups = (
            (highest(s0[...], two[0:2], five[0:2], eight[0:2]), 0),
            (highest(s1[...], two[2:4], five[2:4], eight[2:4]), sign),
            (highest(two[4:6], five[4:6], eight[4:6]), -sign),
            (highest(s3[...], five[6:8], eight[6:8]), 2 * sign),
            (highest(s4[...], five[8:10], eight[8:10]), -2 * sign),
            (highest(s7[...], eight[10:12]), 3 * sign),
            (highest(s6[...], eight[12:14]), -3 * sign),
            (s9, 4),
        )
        for k, (rows, step) in enumerate(groups):
            for j in range(2):
                which = me if (j == 0) != (k in (2, 4, 6)) else 1 - me
                out[pl.ds(which * 8 + lax.rem(level + step + 16, 8), 1), :] = rows[j : j + 1]

    scores = (s0, s1, s2, s3, s4, s5, s6, s7, s8)
    partial = score([(r4, base + near_a + near_b + opposite)], "s9", extra=scores, finish=merge_body)
    returned = lax.all_to_all(partial, ("core", "z"), split_axis=0, concat_axis=0, tiled=True)
    return jnp.max(returned, axis=0)


def solution(mesh):
    fine = Mesh(mesh.devices.reshape(SIZES), AXES)
    return jax.shard_map(
        on_device,
        mesh=fine,
        in_specs=(P(AXES, None), P(AXES, None), P(AXES)),
        out_specs=P(AXES),
        check_vma=False,
    )
```
